128 devices in a mesh: pool: 2 (over z_hi), grp: 8 (over x, core), tp: 8 (over z_lo, y).
Axes of the slice: x: 4, y: 4, z: 4 (z_hi: 2, z_lo: 2; z = z_hi * 2 + z_lo), core: 2. Of those that a mesh axis runs over, the one named last changes fastest.
Arguments:
- query: bfloat16 [512, 8192], P(('pool', 'grp'), 'tp'), may hold values from -6 to 6
- new_kv: bfloat16 [2, 512, 1024], P(None, ('pool', 'grp'), 'tp'), may hold values from -8 to 8
- cache: bfloat16 [2, 512, 8, 256, 128], P(None, ('pool', 'grp'), 'tp'), may hold values from -12 to 12
- lengths: int32 [512], P(('pool', 'grp')), may hold values from 1 to 256, as said below
- out_weight: bfloat16 [8192, 16384], P('tp', ('pool', 'grp')), may hold values from -0.125 to 0.125
- residual: bfloat16 [512, 16384], P('tp', ('pool', 'grp')), may hold values from -20 to 20
- norm_gain: float32 [16384], P(('pool', 'grp')), may hold values from 0.1 to 1.9
- gate_up: bfloat16 [2, 16384, 26624], P(None, ('pool', 'grp'), 'tp'), may hold values from -0.046875 to 0.046875
- down_weight: bfloat16 [26624, 16384], P('tp', ('pool', 'grp')), may hold values from -0.078125 to 0.078125
Outputs:
- layer_out: bfloat16 [512, 16384], P('tp', ('pool', 'grp'))
The draws below stay inside these ranges and needn't reach their ends.
Inputs may be any that keep to these rules, and one draw needn't show every extreme that they name: `lengths`: every row has at least one valid position, and some row has all 256.
All inputs are finite; a program needn't handle non-finite values.
Results may differ from the reference program's by a relative error of at most 0.024.
Values may be sent and summed in bfloat16 or wider, within the bound.
A program may use at most 128 MiB of HBM per device.

```python
import jax
import jax.numpy as jnp
from jax import lax

D = 16384
HEADS = 64
KVH = 8
HD = 128
FF = 26624
LEN = 256
ROWS = 512


def draw_cache(key, part):
    key = jax.random.fold_in(key, 1)
    keys = jnp.clip(jax.random.normal(jax.random.fold_in(key, 1), (ROWS, KVH, LEN, HD), jnp.float32), -6.0, 6.0)
    values = jnp.clip(3.0 * jax.random.normal(jax.random.fold_in(key, 2), (ROWS, KVH, LEN, HD), jnp.float32), -12.0, 12.0)
    return jnp.stack([keys, values]).astype(jnp.bfloat16)


def draw_query(key, part):
    key = jax.random.fold_in(key, 2)
    values = jnp.clip(jax.random.normal(key, (ROWS, HEADS, HD), jnp.float32), -6.0, 6.0)
    return values.reshape(ROWS, HEADS * HD).astype(jnp.bfloat16)


def draw_lengths(key, part):
    key = jax.random.fold_in(key, 3)
    counts = jax.random.randint(jax.random.fold_in(key, 1), (ROWS,), 1, LEN + 1)
    fullrow = jax.random.randint(jax.random.fold_in(key, 2), (), 0, ROWS)
    return jnp.where(jnp.arange(ROWS) == fullrow, LEN, counts).astype(jnp.int32)


def draw_residual(key, part):
    key = jax.random.fold_in(key, 4)
    columns = jnp.arange(D).astype(jnp.float32) / D
    base = jnp.clip(jax.random.normal(jax.random.fold_in(key, 1), (ROWS, D), jnp.float32), -6.0, 6.0)
    values = base * (3.0 ** columns)[None, :]
    return values.astype(jnp.bfloat16)


def block_levels(stream_key, shape, shards, smallest, largest):
    loudness, own = 1.0, jax.random.fold_in(stream_key, 6)
    for position, blocks in shards:
        heights = jnp.exp(jax.random.uniform(jax.random.fold_in(own, position), (blocks,), jnp.float32, smallest / len(shards), largest / len(shards)))
        loudness = loudness * jnp.repeat(heights, shape[position] // blocks).reshape([-1 if axis == position else 1 for axis in range(len(shape))])
    return loudness


def noise(key, extent, spread, reach, cuts=(), dtype=jnp.bfloat16):
    level = block_levels(key, extent, cuts, -0.22, 0.18) if cuts else 1.0
    array = jax.random.normal(key, extent, jnp.float32) * spread * level
    return jnp.minimum(jnp.maximum(array, -reach), reach).astype(dtype)


def setup_inputs(seed: int = 0) -> dict:
    key_list = jax.random.split(jax.random.key(seed), 10)
    query = draw_query(jax.random.fold_in(key_list[9], 71), 0)
    new_kv = noise(key_list[1], (2, ROWS, KVH * HD), 2.0, 8.0, ((1, 16), (2, 8)))
    cache = draw_cache(jax.random.fold_in(key_list[9], 71), 0)
    lengths = draw_lengths(jax.random.fold_in(key_list[9], 71), 0)
    out_weight = noise(key_list[4], (HEADS * HD, D), (HEADS * HD // 4) ** -0.5, 0.125, ((0, 8), (1, 16)))
    residual = draw_residual(jax.random.fold_in(key_list[9], 71), 0)
    norm_gain = jnp.clip(1.0 + 0.18 * jax.random.normal(key_list[6], (D,), jnp.float32), 0.1, 1.9)
    gate_up = noise(key_list[7], (2, D, FF), D ** -0.5, 0.046875, ((1, 16), (2, 8)))
    down_weight = noise(key_list[8], (FF, D), (FF // 4) ** -0.5, 0.078125, ((0, 8), (1, 16)))
    return {"query": query, "new_kv": new_kv, "cache": cache, "lengths": lengths, "out_weight": out_weight, "residual": residual, "norm_gain": norm_gain, "gate_up": gate_up, "down_weight": down_weight}


def attend_row(items):
    q, keys, values, new_key, new_value, length = items
    group = HEADS // KVH
    qg = q.reshape(KVH, group, HD).astype(jnp.float32)
    scale = 1.0 / HD ** 0.5
    scores = jnp.einsum('kgd,kld->kgl', qg, keys.astype(jnp.float32)) * scale
    own = jnp.einsum('kgd,kd->kg', qg, new_key.astype(jnp.float32)) * scale
    valid = jnp.arange(LEN) < length
    scores = jnp.where(valid[None, None, :], scores, -jnp.inf)
    top = jnp.maximum(lax.optimization_barrier(jnp.max(scores, axis=-1)), own)
    expd = jnp.exp(scores - top[..., None])
    exp_own = jnp.exp(own - top)
    total = lax.optimization_barrier(jnp.sum(expd, axis=-1)) + exp_own
    probs = (expd / total[..., None]).astype(jnp.bfloat16)
    prob_own = (exp_own / total).astype(jnp.bfloat16)
    mixed = jnp.einsum('kgl,kld->kgd', probs.astype(jnp.float32), values.astype(jnp.float32))
    mixed = mixed + prob_own.astype(jnp.float32)[..., None] * new_value.astype(jnp.float32)[:, None, :]
    return mixed.reshape(HEADS * HD).astype(jnp.bfloat16)

def reference(query, new_kv, cache, lengths, out_weight, residual, norm_gain, gate_up, down_weight):
    attended = lax.map(attend_row, (query.reshape(ROWS, HEADS, HD), cache[0], cache[1], new_kv[0].reshape(ROWS, KVH, HD), new_kv[1].reshape(ROWS, KVH, HD), lengths))
    hidden_state = residual.astype(jnp.float32) + jnp.dot(attended, out_weight, preferred_element_type=jnp.float32)
    meansq = lax.optimization_barrier(jnp.mean(hidden_state * hidden_state, axis=1))
    normed = (hidden_state * lax.rsqrt(meansq + 1e-05)[:, None] * norm_gain).astype(jnp.bfloat16)
    gate = jnp.dot(normed, gate_up[0], preferred_element_type=jnp.float32)
    upper = jnp.dot(normed, gate_up[1], preferred_element_type=jnp.float32)
    act = (jax.nn.silu(gate) * upper).astype(jnp.bfloat16)
    return (hidden_state + jnp.dot(act, down_weight, preferred_element_type=jnp.float32)).astype(jnp.bfloat16)
```

```python
import jax
import jax.numpy as jnp
from jax import lax
from jax.experimental import pallas as pl
from jax.experimental.pallas import tpu as pltpu
from jax.sharding import PartitionSpec as P

MESH = pl.DeviceIdType.MESH
D = 16384
HD = 128
ROWS = 32
HEADS = 8
SPAN = 256
WIDE = 1024
FF = 3328
TILE = 256
F32 = jnp.float32
BF16 = jnp.bfloat16

A, B = (0, 1, 2), (1, 0, 2)
UNITS = (
    (0, 0, 4, A),
    (0, 4, 3, B),
    (0, 7, 3, A),
    (0, 10, 3, B),
    (1, 0, 4, B),
    (1, 4, 3, A),
    (1, 7, 3, B),
    (1, 10, 3, A),
)
NU = len(UNITS)
LAST = {half: max(u for u in range(NU) if UNITS[u][0] == half) for half in (0, 1)}


def xor_x(x, d):
    if d == 0:
        return x
    if d == 1:
        return x + 1 - 2 * lax.rem(x, 2)
    if d == 2:
        return lax.rem(x + 2, 4)
    return 3 - x


def flip(v, d):
    return 1 - v if d else v


def pick(order, k):
    index = [slice(None)] * 3
    for step in order[:k]:
        index[step] = 0
    index[order[k]] = 1
    return index


def blocks(index):
    out = [()]
    for value in index:
        choices = (0, 1) if isinstance(value, slice) else (value,)
        out = [done + (v,) for done in out for v in choices]
    return out


def within(order, k, bits):
    return tuple(bits[dim] for dim in sorted(order[k + 1 :]))


def body(*refs):
    (lens, query, fresh, residual, gain, cache, out_w, gate_up, down_w, result) = refs[:10]
    (
        qs, ks, vs, outs, kc, vc, ow, gu, dw,
        attall, pbuf, prec, pown, hid, sqall, nall, xp, act, acc, obuf, orec, oown,
    ) = refs[10:32]
    rest = refs[32:]
    parts, crecs, rec0, rec1, rec2 = (rest[i * NU : (i + 1) * NU] for i in range(5))
    (
        load, att_s, att_r, fwd_s, fwd_r, rs1_s, rs1_r, sq_s, sq_r, ag_s, ag_r,
        core_s, core_r, red_s, red_r, gat_s, gat_r, gco_s, gco_r, rs2_s, rs2_r,
    ) = rest[5 * NU :]
    recs = (rec0, rec1, rec2)

    p, g, t = lax.axis_index("pool"), lax.axis_index("grp"), lax.axis_index("tp")
    x, c = lax.div(g, 2), lax.rem(g, 2)
    zl, y = lax.div(t, 4), lax.rem(t, 4)

    def peer(dc, dx, dz):
        return (flip(p, dz), xor_x(x, dx) * 2 + flip(c, dc), t)

    def tp_of(d):
        return flip(zl, d // 4) * 4 + xor_x(y, d % 4)

    def tp_peer(d):
        return (p, g, tp_of(d))

    step_peer = (peer(0, 1, 0), peer(0, 3, 0), peer(0, 0, 1))
    others = [(dc, dx, dz) for dz in (0, 1) for dx in range(4) for dc in (0, 1)][1:]

    def remote(src, dst, send, recv, device):
        copy = pltpu.make_async_remote_copy(
            src_ref=src, dst_ref=dst, send_sem=send, recv_sem=recv, device_id=device, device_id_type=MESH
        )
        copy.start()
        return copy

    barrier = pltpu.get_barrier_semaphore()
    for other in others:
        pl.semaphore_signal(barrier, inc=1, device_id=peer(*other), device_id_type=MESH)
    for d in range(1, 8):
        pl.semaphore_signal(barrier, inc=1, device_id=tp_peer(d), device_id_type=MESH)

    loads = []

    def fetch(src, dst):
        copy = pltpu.make_async_copy(src, dst, load.at[len(loads)])
        copy.start()
        loads.append(copy)
        return copy

    caches = []
    for i in range(4):
        rows = pl.ds(i * 8, 8)
        caches.append((fetch(cache.at[0, rows, 0], kc.at[rows]), fetch(cache.at[1, rows, 0], vc.at[rows])))
    got_ow = fetch(out_w, ow)
    got_gu = [fetch(gate_up.at[k, pl.ds(i * 512, 512)], gu.at[k, pl.ds(i * 512, 512)]) for k in (0, 1) for i in (0, 1)]
    got_dw = [fetch(down_w.at[pl.ds(i * 1664, 1664)], dw.at[pl.ds(i * 1664, 1664)]) for i in (0, 1)]

    scale = 1.0 / HD**0.5
    fresh_k, fresh_v = fresh[0].astype(F32), fresh[1].astype(F32)
    for h in range(HEADS):
        qs[:, h, :] = query[:, h * HD : (h + 1) * HD].astype(F32)
        ks[:, h, :] = fresh_k
        vs[:, h, :] = fresh_v
    place = lax.broadcasted_iota(jnp.int32, (HEADS, SPAN), 1)
    for i in range(4):
        for copy in caches[i]:
            copy.wait()
        rows = range(i * 8, i * 8 + 8)
        scores, own = [], []
        for r in rows:
            q = qs[r]
            s = lax.dot_general(q.astype(BF16), kc[r], (((1,), (1,)), ((), ())), preferred_element_type=F32)
            scores.append(jnp.where(place < lens[r], s * scale, -jnp.inf))
            own.append(jnp.sum(q * ks[r], axis=1, keepdims=True) * scale)
        scores, own = jnp.concatenate(scores, axis=0), jnp.concatenate(own, axis=0)
        top = jnp.maximum(jnp.max(scores, axis=1, keepdims=True), own)
        expd, exp_own = jnp.exp(scores - top), jnp.exp(own - top)
        total = jnp.sum(expd, axis=1, keepdims=True) + exp_own
        probs = (expd / total).astype(BF16).astype(F32)
        prob_own = (exp_own / total).astype(BF16).astype(F32)
        for n, r in enumerate(rows):
            part = slice(n * HEADS, (n + 1) * HEADS)
            mixed = jnp.dot(probs[part].astype(BF16), vc[r], preferred_element_type=F32)
            outs[r] = mixed + prob_own[part] * vs[r]
    mine = g + 8 * p
    for h in range(HEADS):
        attall[mine, :, h * HD : (h + 1) * HD] = outs[:, h, :].astype(BF16)

    pl.semaphore_wait(barrier, 22)
    pending = []
    direct = [(dx, dz) for dz in (1, 0) for dx in (2, 1, 3, 0)][:-1]
    for n, (dx, dz) in enumerate(direct):
        pending.append(remote(attall.at[mine], attall.at[mine], att_s.at[n], att_r.at[n], peer(0, dx, dz)))
    pending.append(remote(attall.at[mine], attall.at[mine], fwd_s.at[7], fwd_r.at[7], peer(1, 0, 0)))
    forwards = [pending[7]]
    for n in (5, 4, 6, 3, 1, 2, 0):
        dx, dz = direct[n]
        pending[n].wait_recv()
        block = flip(p, dz) * 8 + xor_x(x, dx) * 2 + c
        forwards.append(remote(attall.at[block], attall.at[block], fwd_s.at[n], fwd_r.at[n], peer(1, 0, 0)))
    for copy in forwards:
        copy.wait_recv()
    pending += forwards[1:]

    got_ow.wait()
    half_t = lax.div(t, 2)
    for dd in (2, 3, 1, 0):
        j = flip(lax.div(half_t, 2), dd // 2) * 2 + flip(lax.rem(half_t, 2), dd % 2)
        rows = jnp.concatenate([attall[4 * j + i] for i in range(4)], axis=0)
        for n in range(WIDE // TILE):
            cols = slice(n * TILE, (n + 1) * TILE)
            prod = jnp.dot(rows, ow[:, cols], preferred_element_type=F32)
            for i in range(2):
                pbuf[2 * j + i, :, cols] = prod[i * 64 : (i + 1) * 64].astype(BF16)
                if dd == 0:
                    pown[i, :, cols] = prod[i * 64 : (i + 1) * 64]
        for d in (2 * dd, 2 * dd + 1):
            if d:
                pending.append(
                    remote(pbuf.at[tp_of(d)], prec.at[d - 1], rs1_s.at[d - 1], rs1_r.at[d - 1], tp_peer(d))
                )
    sums = pending[-7:]
    for copy in sums:
        copy.wait_recv()
    mine_t = lax.rem(t, 2)
    squares = []
    for n in range(4):
        cols = slice(n * TILE, (n + 1) * TILE)
        total = residual[:, cols].astype(F32) + pown[mine_t, :, cols]
        for d in range(7):
            total = total + prec[d, :, cols].astype(F32)
        hid[:, cols] = total
        squares.append(jnp.sum(total * total, axis=1, keepdims=True))
    square = squares[0] + squares[1] + squares[2] + squares[3]

    wide = jnp.broadcast_to(square, (64, 128))
    sqall[0] = jnp.concatenate([wide, wide], axis=0).T[:8]
    exchanged = []
    for n, other in enumerate(others):
        exchanged.append(remote(sqall.at[0], sqall.at[n + 1], sq_s.at[n], sq_r.at[n], peer(*other)))
    for copy in exchanged:
        copy.wait_recv()
    pending += exchanged
    total = sqall[0]
    for n in range(15):
        total = total + sqall[n + 1]
    factor = lax.rsqrt(total / D + 1e-05)
    factor = jnp.broadcast_to(factor[:1], (128, 128)).T[:64]
    for n in range(WIDE // 128):
        cols = slice(n * 128, (n + 1) * 128)
        normed = (hid[:, cols] * factor * gain[:, cols]).astype(BF16)
        for i in range(4):
            nall[i, :, cols] = normed[i * 16 : (i + 1) * 16]

    gathers = [None]
    for d in (1, 3, 2, 4, 5, 7, 6):
        gathers.append(
            remote(nall.at[pl.ds(0, 4)], nall.at[pl.ds(4 * d, 4)], ag_s.at[d - 1], ag_r.at[d - 1], tp_peer(d))
        )
    pending += gathers[1:]

    def owner(ic, i1, i3, iz):
        return flip(c, ic) * 8 + xor_x(x, i1 ^ (3 * i3)) * 2 + flip(p, iz)

    rels = [(ic, i1, i3, iz) for ic in (0, 1) for i1 in (0, 1) for i3 in (0, 1) for iz in (0, 1)]

    def arrange(half):
        for copy in gathers[1:4] if half == 0 else gathers[4:]:
            copy.wait_recv()
        for n, rel in enumerate(rels):
            xp[half, n] = nall[half * 16 + owner(*rel)]

    def multiply(u):
        half, first, tiles, _ = UNITS[u]
        if u == 0:
            for copy in got_gu:
                copy.wait()
        if first == 0:
            arrange(half)
        width = tiles * TILE
        for k in (0, 1):

            def tile(n, carry, k=k):
                src = pl.ds(pl.multiple_of((first + n) * TILE, TILE), TILE)
                dst = pl.ds(pl.multiple_of(k * width + n * TILE, TILE), TILE)
                rows = xp[half].reshape(256, WIDE)
                prod = jnp.dot(rows, gu[k, :, src], preferred_element_type=F32).astype(BF16)
                parts[u][:, :, :, :, :, dst] = prod.reshape(2, 2, 2, 2, 16, TILE)
                return carry

            lax.fori_loop(0, tiles, tile, 0)
        core_out[u] = remote(parts[u].at[1], crecs[u], core_s.at[u], core_r.at[u], peer(1, 0, 0))

    core_out, red_out, gat_out, gco_out = {}, {}, {}, {}

    def summed(u, k, bits, cols):
        order = UNITS[u][3]
        total = parts[u][(0,) + bits + (slice(None), cols)].astype(F32)
        total = total + crecs[u][bits + (slice(None), cols)].astype(F32)
        for j in range(k):
            total = total + recs[j][u][within(order, j, bits) + (slice(None), cols)].astype(F32)
        return total

    def reduce_step(u, k):
        _, _, tiles, order = UNITS[u]
        if k == 0:
            core_out[u].wait_recv()
        else:
            red_out[u, k - 1].wait_recv()
        index = pick(order, k)
        for bits in blocks(index):
            for n in range(2 * tiles):
                cols = slice(n * TILE, (n + 1) * TILE)
                parts[u][(0,) + bits + (slice(None), cols)] = summed(u, k, bits, cols).astype(BF16)
        red_out[u, k] = remote(
            parts[u].at[(0, *index)], recs[k][u], red_s.at[u, k], red_r.at[u, k], step_peer[order[k]]
        )

    def gather_index(u, k, bit):
        _, first, tiles, order = UNITS[u]
        index = [slice(None)] * 3
        for step in order[:k]:
            index[step] = 0
        index[order[k]] = bit
        return tuple(index) + (slice(None), pl.ds(first * TILE, tiles * TILE))

    def gather_step(u, k):
        half, first, tiles, order = UNITS[u]
        if k == 2:
            red_out[u, 2].wait_recv()
            width = tiles * TILE
            for n in range(tiles):
                gate = summed(u, 3, (0, 0, 0), slice(n * TILE, (n + 1) * TILE))
                up = summed(u, 3, (0, 0, 0), slice(width + n * TILE, width + (n + 1) * TILE))
                cols = slice((first + n) * TILE, (first + n + 1) * TILE)
                act[half, 0, 0, 0, 0, :, cols] = (gate / (1.0 + jnp.exp(-gate)) * up).astype(BF16)
        else:
            gat_out[u, k + 1].wait_recv()
        gat_out[u, k] = remote(
            act.at[(half, 0, *gather_index(u, k, 0))],
            act.at[(half, 0, *gather_index(u, k, 1))],
            gat_s.at[u, k],
            gat_r.at[u, k],
            step_peer[order[k]],
        )

    def gather_core(u):
        half, first, tiles, _ = UNITS[u]
        gat_out[u, 0].wait_recv()
        index = (slice(None),) * 4 + (pl.ds(first * TILE, tiles * TILE),)
        gco_out[u] = remote(
            act.at[(half, 0, *index)], act.at[(half, 1, *index)], gco_s.at[u], gco_r.at[u], peer(1, 0, 0)
        )

    final = []

    def down(u):
        half, first, tiles, _ = UNITS[u]
        gco_out[u].wait_recv()
        if u == 0:
            for copy in got_dw:
                copy.wait()
        width = tiles * TILE
        span = pl.ds(first * TILE, width)

        def tile(n, carry):
            cols = pl.ds(pl.multiple_of(n * TILE, TILE), TILE)
            rows = act[half, :, :, :, :, :, span].reshape(256, width)
            prod = jnp.dot(rows, dw[span, cols], preferred_element_type=F32)
            if first:
                prod = prod + acc[half, :, cols]
            acc[half, :, cols] = prod
            return carry

        lax.fori_loop(0, WIDE // TILE, tile, 0)
        if u == LAST[half]:
            for n, rel in enumerate(rels):
                block = acc[half, n * 16 : (n + 1) * 16]
                obuf[half * 16 + owner(*rel)] = block.astype(BF16)
                if half == 0:
                    oown[owner(*rel)] = block
            for d in (2, 1, 3) if half == 0 else (6, 5, 7, 4):
                final.append(
                    remote(obuf.at[pl.ds(4 * d, 4)], orec.at[d - 1], rs2_s.at[d - 1], rs2_r.at[d - 1], tp_peer(d))
                )

    actions = (
        multiply,
        lambda u: reduce_step(u, 0),
        lambda u: reduce_step(u, 1),
        lambda u: reduce_step(u, 2),
        lambda u: gather_step(u, 2),
        lambda u: gather_step(u, 1),
        lambda u: gather_step(u, 0),
        gather_core,
        down,
    )
    for wave in range(NU + len(actions) - 1):
        for u in range(NU):
            if 0 <= wave - u < len(actions):
                actions[wave - u](u)

    for copy in final:
        copy.wait_recv()
    for i in range(4):
        for n in range(WIDE // TILE):
            cols = slice(n * TILE, (n + 1) * TILE)
            total = hid[i * 16 : (i + 1) * 16, cols] + oown[i, :, cols]
            for d in range(7):
                total = total + orec[d, i, :, cols].astype(F32)
            result[i * 16 : (i + 1) * 16, cols] = total.astype(BF16)

    for copies in (core_out, red_out, gat_out, gco_out):
        pending.extend(copies.values())
    for copy in pending + final:
        copy.wait_send()


def on_device(query, new_kv, cache, lengths, out_weight, residual, norm_gain, gate_up, down_weight):
    vmem, smem, hbm = (pl.BlockSpec(memory_space=s) for s in (pltpu.VMEM, pltpu.SMEM, pl.ANY))
    dma = pltpu.SemaphoreType.DMA
    widths = [2 * TILE * tiles for _, _, tiles, _ in UNITS]
    scratch = [
        pltpu.VMEM((ROWS, HEADS, HD), F32),
        pltpu.VMEM((ROWS, HEADS, HD), F32),
        pltpu.VMEM((ROWS, HEADS, HD), F32),
        pltpu.VMEM((ROWS, HEADS, HD), F32),
        pltpu.VMEM((ROWS, SPAN, HD), BF16),
        pltpu.VMEM((ROWS, SPAN, HD), BF16),
        pltpu.VMEM((1024, WIDE), BF16),
        pltpu.VMEM((2, WIDE, FF), BF16),
        pltpu.VMEM((FF, WIDE), BF16),
        pltpu.VMEM((16, 32, 1024), BF16),
        pltpu.VMEM((8, 64, WIDE), BF16),
        pltpu.VMEM((7, 64, WIDE), BF16),
        pltpu.VMEM((2, 64, WIDE), F32),
        pltpu.VMEM((64, WIDE), F32),
        pltpu.VMEM((16, 8, 128), F32),
        pltpu.VMEM((32, 16, WIDE), BF16),
        pltpu.VMEM((2, 16, 16, WIDE), BF16),
        pltpu.VMEM((2, 2, 2, 2, 2, 16, FF), BF16),
        pltpu.VMEM((2, 256, WIDE), F32),
        pltpu.VMEM((32, 16, WIDE), BF16),
        pltpu.VMEM((7, 4, 16, WIDE), BF16),
        pltpu.VMEM((16, 16, WIDE), F32),
    ]
    scratch += [pltpu.VMEM((2, 2, 2, 2, 16, w), BF16) for w in widths]
    scratch += [pltpu.VMEM((2, 2, 2, 16, w), BF16) for w in widths]
    scratch += [pltpu.VMEM((2, 2, 16, w), BF16) for w in widths]
    scratch += [pltpu.VMEM((2, 16, w), BF16) for w in widths]
    scratch += [pltpu.VMEM((16, w), BF16) for w in widths]
    scratch += [dma((16,))]
    for shape in ((7,), (8,), (7,), (15,), (7,), (NU,), (NU, 3), (NU, 3), (NU,), (7,)):
        scratch += [dma(shape), dma(shape)]
    return pl.pallas_call(
        body,
        out_shape=jax.ShapeDtypeStruct((64, WIDE), BF16),
        in_specs=[smem, vmem, vmem, vmem, vmem, hbm, hbm, hbm, hbm],
        out_specs=vmem,
        scratch_shapes=scratch,
        compiler_params=pltpu.CompilerParams(
            collective_id=0, has_side_effects=True, vmem_limit_bytes=63 * 2**20
        ),
        cost_estimate=pl.CostEstimate(flops=11_600_000_000, bytes_accessed=27_000_000, transcendentals=1_000_000),
    )(lengths, query, new_kv, residual, norm_gain.reshape(1, WIDE), cache, out_weight, gate_up, down_weight)


def solution(mesh):
    in_specs = (
        P(("pool", "grp"), "tp"),
        P(None, ("pool", "grp"), "tp"),
        P(None, ("pool", "grp"), "tp", None, None),
        P(("pool", "grp")),
        P("tp", ("pool", "grp")),
        P("tp", ("pool", "grp")),
        P(("pool", "grp")),
        P(None, ("pool", "grp"), "tp"),
        P("tp", ("pool", "grp")),
    )
    return jax.shard_map(
        on_device, mesh=mesh, in_specs=in_specs, out_specs=P("tp", ("pool", "grp")), check_vma=False
    )
```

```python
import jax
import jax.numpy as jnp
from jax import lax
from jax.experimental import pallas as pl
from jax.experimental.pallas import tpu as pltpu
from jax.sharding import PartitionSpec as P

MESH = pl.DeviceIdType.MESH
D = 16384
HD = 128
ROWS = 32
HEADS = 8
SPAN = 256
WIDE = 1024
FF = 3328
TILE = 256
F32 = jnp.float32
BF16 = jnp.bfloat16

LANES = 128
A, B = (0, 1), (1, 0)
QUARTERS = 4
UNITS = (
    (0, 0, 14, A),
    (0, 14, 12, B),
    (1, 0, 14, B),
    (1, 14, 12, A),
    (2, 0, 14, A),
    (2, 14, 12, B),
    (3, 0, 14, B),
    (3, 14, 12, A),
)
NU = len(UNITS)
FIRST = {q: min(u for u in range(NU) if UNITS[u][0] == q) for q in range(QUARTERS)}


ORDER = (1, 2, 0, 3, 4, 5, 6, 7)


def xor_x(x, d):
    if d == 0:
        return x
    if d == 1:
        return x + 1 - 2 * lax.rem(x, 2)
    if d == 2:
        return lax.rem(x + 2, 4)
    return 3 - x


def flip(v, d):
    return 1 - v if d else v


def pick(order, k, bit=1):
    index = [slice(None)] * 2
    for step in order[:k]:
        index[step] = 0
    index[order[k]] = bit
    return tuple(index)


def blocks(index):
    out = [()]
    for value in index:
        choices = (0, 1) if isinstance(value, slice) else (value,)
        out = [done + (v,) for done in out for v in choices]
    return out


def pieces(first, count):
    return [(first + n, min(2, count - n)) for n in range(0, count, 2)]


def lanes(first, count):
    return slice(first * LANES, (first + count) * LANES)


def body(*refs):
    (lens, query, fresh, residual, gain, cache, out_w, gate_up, down_w, result) = refs[:10]
    (
        qs, ks, vs, outs, kc, vc, ow, gu, dw, attall, pbuf, prec, hid,
        sqall, fall, nall, xp, act, obuf, orec,
    ) = refs[10:30]
    rest = refs[30:]
    parts, crecs, rec0, rec1, rec2 = (rest[i * NU : (i + 1) * NU] for i in range(5))
    (
        load, att_s, att_r, fwd_s, fwd_r, rs1_s, rs1_r, sq_s, sq_r, fac_s, fac_r, ag_s, ag_r,
        core_s, core_r, red_s, red_r, gat_s, gat_r, gco_s, gco_r, rs2_s, rs2_r,
    ) = rest[5 * NU :]

    p, g, t = lax.axis_index("pool"), lax.axis_index("grp"), lax.axis_index("tp")
    x, c = lax.div(g, 2), lax.rem(g, 2)
    zl, y = lax.div(t, 4), lax.rem(t, 4)

    def peer(dc, dx, dz):
        return (flip(p, dz), xor_x(x, dx) * 2 + flip(c, dc), t)

    def tp_of(d):
        return flip(zl, d // 4) * 4 + xor_x(y, d % 4)

    def tp_peer(d):
        return (p, g, tp_of(d))

    step_peer = (peer(0, 1, 0), peer(0, 3, 0))
    others = [(dc, dx, dz) for dz in (0, 1) for dx in range(4) for dc in (0, 1)][1:]
    pending = []

    def remote(src, dst, send, recv, device):
        copy = pltpu.make_async_remote_copy(
            src_ref=src, dst_ref=dst, send_sem=send, recv_sem=recv, device_id=device, device_id_type=MESH
        )
        copy.start()
        pending.append(copy)
        return copy

    barrier = pltpu.get_barrier_semaphore()
    for other in others:
        pl.semaphore_signal(barrier, inc=1, device_id=peer(*other), device_id_type=MESH)
    for d in range(1, 8):
        pl.semaphore_signal(barrier, inc=1, device_id=tp_peer(d), device_id_type=MESH)

    loads = []

    def fetch(src, dst):
        copy = pltpu.make_async_copy(src, dst, load.at[len(loads)])
        copy.start()
        loads.append(copy)
        return copy

    caches = []
    for i in range(4):
        rows = pl.ds(i * 8, 8)
        caches.append((fetch(cache.at[0, rows, 0], kc.at[rows]), fetch(cache.at[1, rows, 0], vc.at[rows])))
    got_ow = fetch(out_w, ow)
    got_gu = [fetch(gate_up.at[k, pl.ds(i * 512, 512)], gu.at[k, pl.ds(i * 512, 512)]) for k in (0, 1) for i in (0, 1)]
    got_dw = [fetch(down_w.at[pl.ds(i * 1664, 1664)], dw.at[pl.ds(i * 1664, 1664)]) for i in (0, 1)]

    scale = 1.0 / HD**0.5
    fresh_k, fresh_v = fresh[0].astype(F32), fresh[1].astype(F32)
    for h in range(HEADS):
        qs[:, h, :] = query[:, h * HD : (h + 1) * HD].astype(F32)
        ks[:, h, :] = fresh_k
        vs[:, h, :] = fresh_v
    place = lax.broadcasted_iota(jnp.int32, (HEADS, SPAN), 1)
    mine = p * 4 + x

    def attend(i):
        for copy in caches[i]:
            copy.wait()
        rows = range(i * 8, i * 8 + 8)
        scores, own = [], []
        for r in rows:
            q = qs[r]
            s = lax.dot_general(q.astype(BF16), kc[r], (((1,), (1,)), ((), ())), preferred_element_type=F32)
            scores.append(jnp.where(place < lens[r], s * scale, -jnp.inf))
            own.append(jnp.sum(q * ks[r], axis=1, keepdims=True) * scale)
        scores, own = jnp.concatenate(scores, axis=0), jnp.concatenate(own, axis=0)
        top = jnp.maximum(jnp.max(scores, axis=1, keepdims=True), own)
        expd, exp_own = jnp.exp(scores - top), jnp.exp(own - top)
        total = jnp.sum(expd, axis=1, keepdims=True) + exp_own
        probs = (expd / total).astype(BF16).astype(F32)
        prob_own = (exp_own / total).astype(BF16).astype(F32)
        for n, r in enumerate(rows):
            part = slice(n * HEADS, (n + 1) * HEADS)
            mixed = jnp.dot(probs[part].astype(BF16), vc[r], preferred_element_type=F32)
            outs[r] = mixed + prob_own[part] * vs[r]

    direct = [(dx, dz) for dz in (1, 0) for dx in (2, 1, 3, 0)][:-1]
    spread = {}

    def attention(half):
        attend(2 * half)
        attend(2 * half + 1)
        for h in range(HEADS):
            attall[half, c, mine, :, h * HD : (h + 1) * HD] = outs[half * 16 : half * 16 + 16, h, :].astype(BF16)
        if half == 0:
            pl.semaphore_wait(barrier, 22)
        block = attall.at[half, c, mine]
        spread[half] = [
            remote(block, block, att_s.at[half, n], att_r.at[half, n], peer(0, *direct[n])) for n in range(7)
        ]
        spread[half].append(remote(block, block, fwd_s.at[half, 7], fwd_r.at[half, 7], peer(1, 0, 0)))

    def pass_on(half):
        forwards = [spread[half][7]]
        for n in (5, 4, 6, 3, 1, 2, 0):
            dx, dz = direct[n]
            spread[half][n].wait_recv()
            block = attall.at[half, c, flip(p, dz) * 4 + xor_x(x, dx)]
            forwards.append(remote(block, block, fwd_s.at[half, n], fwd_r.at[half, n], peer(1, 0, 0)))
        for copy in forwards:
            copy.wait_recv()

    sums = {}

    def project(q):
        rows = attall[q // 2, q % 2].reshape(128, 1024)
        for n in range(WIDE // TILE):
            cols = slice(n * TILE, (n + 1) * TILE)
            prod = jnp.dot(rows, ow[:, cols], preferred_element_type=F32)
            pbuf[q, :, :, cols] = prod.astype(BF16).reshape(8, 16, TILE)
        sums[q] = [
            remote(pbuf.at[q, tp_of(d)], prec.at[q, d - 1], rs1_s.at[q, d - 1], rs1_r.at[q, d - 1], tp_peer(d))
            for d in (6, 4, 2, 5, 7, 1, 3)
        ]

    gathers, squares = {}, {}

    def rows_of(q):
        first = q % 2 * 32 + q // 2 * 16
        return slice(first, first + 16)

    def add_up(q):
        for copy in sums[q]:
            copy.wait_recv()
        square = 0.0
        for n in range(WIDE // TILE):
            cols = slice(n * TILE, (n + 1) * TILE)
            total = residual[rows_of(q), cols].astype(F32) + pbuf[q, t, :, cols].astype(F32)
            for d in range(7):
                total = total + prec[q, d, :, cols].astype(F32)
            hid[q, :, cols] = total
            square = square + jnp.sum(total * total, axis=1, keepdims=True)
            nall[q, 0, :, cols] = (total * gain[:, cols]).astype(BF16)
        squares[q] = square
        gathers[q] = [
            remote(nall.at[q, 0], nall.at[q, d], ag_s.at[q, d - 1], ag_r.at[q, d - 1], tp_peer(d))
            for d in (6, 4, 2, 5, 7, 1, 3)
        ]

    square_copies, factor_copies = {}, {}

    def share_squares(half):
        both = [jnp.broadcast_to(squares[2 * half + e], (16, 128)) for e in (0, 1)]
        sqall[half, 0] = jnp.concatenate(both * 4, axis=0).T[:8]
        square_copies[half] = [
            remote(sqall.at[half, 0], sqall.at[half, n + 1], sq_s.at[half, n], sq_r.at[half, n], peer(*other))
            for n, other in enumerate(others)
        ]

    def share_factor(half):
        for copy in square_copies[half]:
            copy.wait_recv()
        total = sqall[half, 0]
        for n in range(15):
            total = total + sqall[half, n + 1]
        fall[half, 0] = lax.rsqrt(total / D + 1e-05)
        factor_copies[half] = [
            remote(fall.at[half, 0], fall.at[half, d], fac_s.at[half, d - 1], fac_r.at[half, d - 1], tp_peer(d))
            for d in range(1, 8)
        ]

    rels = [(ic, i1, i3) for ic in (0, 1) for i1 in (0, 1) for i3 in (0, 1)]

    def owner(ic, i1, i3):
        return flip(c, ic) * 4 + xor_x(x, i1 ^ (3 * i3))

    def arrange(q):
        for copy in gathers[q]:
            copy.wait_recv()
        for n, rel in enumerate(rels):
            xp[q, n] = nall[q, owner(*rel)]

    core_out, red_out, gat_out, gco_out = {}, {}, {}, {}
    factors, final = {}, {}

    def multiply(u):
        q, first, count, _ = UNITS[u]
        if u == 0:
            for copy in got_gu:
                copy.wait()
        if u == FIRST[q]:
            arrange(q)
        rows = xp.at[q]
        for k in (0, 1):

            def tile(src, dst, width, k=k):
                prod = jnp.dot(rows[...].reshape(128, WIDE), gu[k, :, pl.ds(src, width)], preferred_element_type=F32)
                parts[u][:, :, :, :, pl.ds(dst, width)] = prod.astype(BF16).reshape(2, 2, 2, 16, width)

            def step(n, carry, k=k, tile=tile):
                src = pl.multiple_of(first * LANES + n * TILE, LANES)
                tile(src, pl.multiple_of(k * count * LANES + n * TILE, LANES), TILE)
                return carry

            lax.fori_loop(0, count // 2, step, 0, unroll=True)
            if count % 2:
                tile((first + count - 1) * LANES, (k * count + count - 1) * LANES, LANES)
        core_out[u] = remote(parts[u].at[1], crecs[u], core_s.at[u], core_r.at[u], peer(1, 0, 0))

    def summed(u, k, bits, cols):
        order = UNITS[u][3]
        total = parts[u][(0, *bits, slice(None), cols)].astype(F32)
        total = total + crecs[u][(*bits, slice(None), cols)].astype(F32)
        if k > 0:
            total = total + rec0[u][bits[order[1]], :, cols].astype(F32)
        if k > 1:
            total = total + rec1[u][:, cols].astype(F32)
        return total

    def reduce_step(u, k):
        _, _, count, order = UNITS[u]
        if k == 0:
            core_out[u].wait_recv()
        else:
            red_out[u, k - 1].wait_recv()
        index = pick(order, k) if k < 2 else (0, 0)
        for bits in blocks(index):
            for first, n in pieces(0, 2 * count):
                cols = lanes(first, n)
                total = summed(u, k, bits, cols)
                parts[u][(0, *bits, slice(None), cols)] = total.astype(BF16)
        device = step_peer[order[k]] if k < 2 else peer(0, 0, 1)
        red_out[u, k] = remote(
            parts[u].at[(0, *index)], (rec0, rec1, rec2)[k][u], red_s.at[u, k], red_r.at[u, k], device
        )

    def factor(q):
        half = q // 2
        if half not in factors:
            for copy in factor_copies[half]:
                copy.wait_recv()
            factors[half] = jnp.broadcast_to(fall[half, owner(0, 0, 0)][:1], (128, 128)).T
        return factors[half][q % 2 * 16 : q % 2 * 16 + 16]

    def activate(u):
        q, first, count, order = UNITS[u]
        red_out[u, 2].wait_recv()
        scales = factor(q)
        for n in range(count):
            gate, up = (
                (parts[u][0, 0, 0, :, lanes(n + k * count, 1)].astype(F32) + rec2[u][:, lanes(n + k * count, 1)].astype(F32))
                * scales
                for k in (0, 1)
            )
            act[q, 0, 0, 0, :, lanes(first + n, 1)] = (gate / (1.0 + jnp.exp(-gate)) * up).astype(BF16)
        gather_step(u, 1)

    def gather_step(u, k):
        q, first, count, order = UNITS[u]
        if k == 0:
            gat_out[u, 1].wait_recv()
        cols = pl.ds(first * LANES, count * LANES)
        gat_out[u, k] = remote(
            act.at[(q, 0, *pick(order, k, 0), slice(None), cols)],
            act.at[(q, 0, *pick(order, k, 1), slice(None), cols)],
            gat_s.at[u, k],
            gat_r.at[u, k],
            step_peer[order[k]],
        )

    def gather_core(u):
        q, first, count, _ = UNITS[u]
        gat_out[u, 0].wait_recv()
        index = (slice(None),) * 3 + (pl.ds(first * LANES, count * LANES),)
        gco_out[u] = remote(
            act.at[(q, 0, *index)], act.at[(q, 1, *index)], gco_s.at[u], gco_r.at[u], peer(1, 0, 0)
        )

    def down(q):
        for u in range(NU):
            if UNITS[u][0] == q:
                gco_out[u].wait_recv()
        if q == 0:
            for copy in got_dw:
                copy.wait()

        def tile(n, carry):
            cols = pl.ds(pl.multiple_of(n * TILE, TILE), TILE)
            prod = jnp.dot(act[q].reshape(128, FF), dw[:, cols], preferred_element_type=F32).astype(BF16)
            for i, rel in enumerate(rels):
                obuf[q, owner(*rel), :, cols] = prod[i * 16 : (i + 1) * 16]
            return carry

        lax.fori_loop(0, WIDE // TILE, tile, 0, unroll=True)
        final[q] = [
            remote(obuf.at[q, d], orec.at[q, d - 1], rs2_s.at[q, d - 1], rs2_r.at[q, d - 1], tp_peer(d))
            for d in (6, 4, 2, 5, 7, 1, 3)
        ]

    def finish(q):
        for copy in final[q]:
            copy.wait_recv()
        for n in range(WIDE // TILE):
            cols = slice(n * TILE, (n + 1) * TILE)
            total = hid[q, :, cols] + obuf[q, 0, :, cols].astype(F32)
            for d in range(7):
                total = total + orec[q, d, :, cols].astype(F32)
            result[rows_of(q), cols] = total.astype(BF16)

    attention(0)
    attention(1)
    pass_on(0)
    got_ow.wait()
    project(0)
    project(1)
    pass_on(1)
    project(2)
    add_up(0)
    project(3)
    add_up(1)
    share_squares(0)
    add_up(2)
    actions = (
        multiply,
        lambda u: reduce_step(u, 0),
        lambda u: reduce_step(u, 1),
        lambda u: reduce_step(u, 2),
        activate,
        lambda u: gather_step(u, 0),
        gather_core,
    )
    for wave in range(QUARTERS + len(actions)):
        for n in ORDER:
            q = wave - n
            if 0 <= q < QUARTERS:
                if n < len(actions):
                    actions[n](2 * q)
                    actions[n](2 * q + 1)
                else:
                    down(q)
        if wave == 0:
            add_up(3)
            share_squares(1)
            share_factor(0)
        if wave == 1:
            share_factor(1)
    for q in range(QUARTERS):
        finish(q)
    for copy in pending:
        copy.wait_send()


def on_device(query, new_kv, cache, lengths, out_weight, residual, norm_gain, gate_up, down_weight):
    vmem, smem, hbm = (pl.BlockSpec(memory_space=s) for s in (pltpu.VMEM, pltpu.SMEM, pl.ANY))
    dma = pltpu.SemaphoreType.DMA
    widths = [2 * LANES * count for _, _, count, _ in UNITS]
    scratch = [
        pltpu.VMEM((ROWS, HEADS, HD), F32),
        pltpu.VMEM((ROWS, HEADS, HD), F32),
        pltpu.VMEM((ROWS, HEADS, HD), F32),
        pltpu.VMEM((ROWS, HEADS, HD), F32),
        pltpu.VMEM((ROWS, SPAN, HD), BF16),
        pltpu.VMEM((ROWS, SPAN, HD), BF16),
        pltpu.VMEM((1024, WIDE), BF16),
        pltpu.VMEM((2, WIDE, FF), BF16),
        pltpu.VMEM((FF, WIDE), BF16),
        pltpu.VMEM((2, 2, 8, 16, 1024), BF16),
        pltpu.VMEM((QUARTERS, 8, 16, WIDE), BF16),
        pltpu.VMEM((QUARTERS, 7, 16, WIDE), BF16),
        pltpu.VMEM((QUARTERS, 16, WIDE), F32),
        pltpu.VMEM((2, 16, 8, 128), F32),
        pltpu.VMEM((2, 8, 8, 128), F32),
        pltpu.VMEM((QUARTERS, 8, 16, WIDE), BF16),
        pltpu.VMEM((QUARTERS, 8, 16, WIDE), BF16),
        pltpu.VMEM((QUARTERS, 2, 2, 2, 16, FF), BF16),
        pltpu.VMEM((QUARTERS, 8, 16, WIDE), BF16),
        pltpu.VMEM((QUARTERS, 7, 16, WIDE), BF16),
    ]
    scratch += [pltpu.VMEM((2, 2, 2, 16, w), BF16) for w in widths]
    scratch += [pltpu.VMEM((2, 2, 16, w), BF16) for w in widths]
    scratch += [pltpu.VMEM((2, 16, w), BF16) for w in widths]
    scratch += [pltpu.VMEM((16, w), BF16) for w in widths]
    scratch += [pltpu.VMEM((16, w), BF16) for w in widths]
    scratch += [dma((16,))]
    for shape in (
        (2, 7), (2, 8), (4, 7), (2, 15), (2, 7), (4, 7), (NU,), (NU, 3), (NU, 2), (NU,), (4, 7),
    ):
        scratch += [dma(shape), dma(shape)]
    return pl.pallas_call(
        body,
        out_shape=jax.ShapeDtypeStruct((64, WIDE), BF16),
        in_specs=[smem, vmem, vmem, vmem, vmem, hbm, hbm, hbm, hbm],
        out_specs=vmem,
        scratch_shapes=scratch,
        compiler_params=pltpu.CompilerParams(
            collective_id=0, has_side_effects=True, vmem_limit_bytes=63 * 2**20
        ),
        cost_estimate=pl.CostEstimate(flops=11_600_000_000, bytes_accessed=27_000_000, transcendentals=1_000_000),
    )(lengths, query, new_kv, residual, norm_gain.reshape(1, WIDE), cache, out_weight, gate_up, down_weight)


def solution(mesh):
    in_specs = (
        P(("pool", "grp"), "tp"),
        P(None, ("pool", "grp"), "tp"),
        P(None, ("pool", "grp"), "tp", None, None),
        P(("pool", "grp")),
        P("tp", ("pool", "grp")),
        P("tp", ("pool", "grp")),
        P(("pool", "grp")),
        P(None, ("pool", "grp"), "tp"),
        P("tp", ("pool", "grp")),
    )
    return jax.shard_map(
        on_device, mesh=mesh, in_specs=in_specs, out_specs=P("tp", ("pool", "grp")), check_vma=False
    )
```

```python
import jax
import jax.numpy as jnp
from jax import lax
from jax.experimental import pallas as pl
from jax.experimental.pallas import tpu as pltpu
from jax.sharding import PartitionSpec as P

MESH = pl.DeviceIdType.MESH
D = 16384
HD = 128
ROWS = 32
HEADS = 8
SPAN = 256
WIDE = 1024
FF = 3328
TILE = 256
F32 = jnp.float32
BF16 = jnp.bfloat16

LANES = 128
A, B = (0, 1), (1, 0)
QUARTERS = 4
UNITS = (
    (0, 0, 14, A),
    (0, 14, 12, B),
    (1, 0, 14, B),
    (1, 14, 12, A),
    (2, 0, 14, A),
    (2, 14, 12, B),
    (3, 0, 14, B),
    (3, 14, 12, A),
)
NU = len(UNITS)
FIRST = {q: min(u for u in range(NU) if UNITS[u][0] == q) for q in range(QUARTERS)}


ORDER = (
    ("P", 0), ("P", 2), ("P", 1), ("S", 0), (0, 0), (0, 1), (1, 0), (1, 1), ("P", 3), ("S", 1), (0, 2), (0, 3),
    (1, 2), (1, 3), (0, 4), (0, 5), (2, 0), (2, 1), (1, 4), (1, 5), (0, 6), (0, 7), (2, 2), (3, 0), (2, 3), (3,
    1), (1, 6), (1, 7), (2, 5), (3, 3), ("T", 0), (2, 4), (3, 2), (4, 0), (2, 6), (3, 5), (4, 3), (4, 1), (2, 7),
    (3, 4), (4, 2), (3, 6), (5, 1), (5, 0), ("T", 1), (3, 7), (5, 2), (4, 5), (5, 3), (4, 4), (6, 1), (6, 0), (4,
    6), (4, 7), (6, 3), (6, 2), (5, 4), (5, 5), ("D", 0), (5, 6), (5, 7), ("D", 1), (6, 5), (6, 4), (6, 6), (6,
    7), ("D", 2), ("D", 3), ("F", 2), ("F", 0), ("F", 1), ("F", 3),
)


def xor_x(x, d):
    if d == 0:
        return x
    if d == 1:
        return x + 1 - 2 * lax.rem(x, 2)
    if d == 2:
        return lax.rem(x + 2, 4)
    return 3 - x


def flip(v, d):
    return 1 - v if d else v


def pick(order, k, bit=1):
    index = [slice(None)] * 2
    for step in order[:k]:
        index[step] = 0
    index[order[k]] = bit
    return tuple(index)


def blocks(index):
    out = [()]
    for value in index:
        choices = (0, 1) if isinstance(value, slice) else (value,)
        out = [done + (v,) for done in out for v in choices]
    return out


def pieces(first, count):
    return [(first + n, min(2, count - n)) for n in range(0, count, 2)]


def lanes(first, count):
    return slice(first * LANES, (first + count) * LANES)


def body(*refs):
    (lens, query, fresh, residual, gain, cache, out_w, gate_up, down_w, result) = refs[:10]
    (
        qs, ks, vs, outs, kc, vc, ow, gu, dw, attall, pbuf, prec, hid,
        sqall, fall, nall, xp, act, obuf, orec,
    ) = refs[10:30]
    rest = refs[30:]
    parts, crecs, rec0, rec1, rec2 = (rest[i * NU : (i + 1) * NU] for i in range(5))
    (
        load, att_s, att_r, fwd_s, fwd_r, rs1_s, rs1_r, sq_s, sq_r, fac_s, fac_r, ag_s, ag_r,
        core_s, core_r, red_s, red_r, gat_s, gat_r, gco_s, gco_r, rs2_s, rs2_r,
    ) = rest[5 * NU :]

    p, g, t = lax.axis_index("pool"), lax.axis_index("grp"), lax.axis_index("tp")
    x, c = lax.div(g, 2), lax.rem(g, 2)
    zl, y = lax.div(t, 4), lax.rem(t, 4)

    def peer(dc, dx, dz):
        return (flip(p, dz), xor_x(x, dx) * 2 + flip(c, dc), t)

    def tp_of(d):
        return flip(zl, d // 4) * 4 + xor_x(y, d % 4)

    def tp_peer(d):
        return (p, g, tp_of(d))

    step_peer = (peer(0, 1, 0), peer(0, 3, 0))
    others = [(dc, dx, dz) for dz in (0, 1) for dx in range(4) for dc in (0, 1)][1:]
    pending = []

    def remote(src, dst, send, recv, device):
        copy = pltpu.make_async_remote_copy(
            src_ref=src, dst_ref=dst, send_sem=send, recv_sem=recv, device_id=device, device_id_type=MESH
        )
        copy.start()
        pending.append(copy)
        return copy

    barrier = pltpu.get_barrier_semaphore()
    for other in others:
        pl.semaphore_signal(barrier, inc=1, device_id=peer(*other), device_id_type=MESH)
    for d in range(1, 8):
        pl.semaphore_signal(barrier, inc=1, device_id=tp_peer(d), device_id_type=MESH)

    loads = []

    def fetch(src, dst):
        copy = pltpu.make_async_copy(src, dst, load.at[len(loads)])
        copy.start()
        loads.append(copy)
        return copy

    caches = []
    for i in range(4):
        rows = pl.ds(i * 8, 8)
        caches.append((fetch(cache.at[0, rows, 0], kc.at[rows]), fetch(cache.at[1, rows, 0], vc.at[rows])))
    got_ow = fetch(out_w, ow)
    got_gu = [fetch(gate_up.at[k, pl.ds(i * 512, 512)], gu.at[k, pl.ds(i * 512, 512)]) for k in (0, 1) for i in (0, 1)]
    got_dw = [fetch(down_w.at[pl.ds(i * 1664, 1664)], dw.at[pl.ds(i * 1664, 1664)]) for i in (0, 1)]

    scale = 1.0 / HD**0.5
    fresh_k, fresh_v = fresh[0].astype(F32), fresh[1].astype(F32)
    for h in range(HEADS):
        qs[:, h, :] = query[:, h * HD : (h + 1) * HD].astype(F32)
        ks[:, h, :] = fresh_k
        vs[:, h, :] = fresh_v
    place = lax.broadcasted_iota(jnp.int32, (HEADS, SPAN), 1)
    mine = p * 4 + x

    def attend(i):
        for copy in caches[i]:
            copy.wait()
        rows = range(i * 8, i * 8 + 8)
        scores, own = [], []
        for r in rows:
            q = qs[r]
            s = lax.dot_general(q.astype(BF16), kc[r], (((1,), (1,)), ((), ())), preferred_element_type=F32)
            scores.append(jnp.where(place < lens[r], s * scale, -jnp.inf))
            own.append(jnp.sum(q * ks[r], axis=1, keepdims=True) * scale)
        scores, own = jnp.concatenate(scores, axis=0), jnp.concatenate(own, axis=0)
        top = jnp.maximum(jnp.max(scores, axis=1, keepdims=True), own)
        expd, exp_own = jnp.exp(scores - top), jnp.exp(own - top)
        total = jnp.sum(expd, axis=1, keepdims=True) + exp_own
        probs = (expd / total).astype(BF16).astype(F32)
        prob_own = (exp_own / total).astype(BF16).astype(F32)
        for n, r in enumerate(rows):
            part = slice(n * HEADS, (n + 1) * HEADS)
            mixed = jnp.dot(probs[part].astype(BF16), vc[r], preferred_element_type=F32)
            outs[r] = mixed + prob_own[part] * vs[r]

    direct = [(dx, dz) for dz in (1, 0) for dx in (2, 1, 3, 0)][:-1]
    spread = {}

    def attention(half):
        attend(2 * half)
        attend(2 * half + 1)
        for h in range(HEADS):
            attall[half, c, mine, :, h * HD : (h + 1) * HD] = outs[half * 16 : half * 16 + 16, h, :].astype(BF16)
        if half == 0:
            pl.semaphore_wait(barrier, 22)
        block = attall.at[half, c, mine]
        spread[half] = [
            remote(block, block, att_s.at[half, n], att_r.at[half, n], peer(0, *direct[n])) for n in range(7)
        ]
        spread[half].append(remote(block, block, fwd_s.at[half, 7], fwd_r.at[half, 7], peer(1, 0, 0)))

    def pass_on(half):
        forwards = [spread[half][7]]
        for n in (5, 4, 6, 3, 1, 2, 0):
            dx, dz = direct[n]
            spread[half][n].wait_recv()
            block = attall.at[half, c, flip(p, dz) * 4 + xor_x(x, dx)]
            forwards.append(remote(block, block, fwd_s.at[half, n], fwd_r.at[half, n], peer(1, 0, 0)))
        for copy in forwards:
            copy.wait_recv()

    sums = {}

    def project(q):
        rows = attall[q // 2, q % 2].reshape(128, 1024)
        for n in range(WIDE // TILE):
            cols = slice(n * TILE, (n + 1) * TILE)
            prod = jnp.dot(rows, ow[:, cols], preferred_element_type=F32)
            pbuf[q, :, :, cols] = prod.astype(BF16).reshape(8, 16, TILE)
        sums[q] = [
            remote(pbuf.at[q, tp_of(d)], prec.at[q, d - 1], rs1_s.at[q, d - 1], rs1_r.at[q, d - 1], tp_peer(d))
            for d in (6, 4, 2, 5, 7, 1, 3)
        ]

    gathers, squares = {}, {}

    def rows_of(q):
        first = q % 2 * 32 + q // 2 * 16
        return slice(first, first + 16)

    def add_up(q):
        for copy in sums[q]:
            copy.wait_recv()
        square = 0.0
        for n in range(WIDE // TILE):
            cols = slice(n * TILE, (n + 1) * TILE)
            total = residual[rows_of(q), cols].astype(F32) + pbuf[q, t, :, cols].astype(F32)
            for d in range(7):
                total = total + prec[q, d, :, cols].astype(F32)
            hid[q, :, cols] = total
            square = square + jnp.sum(total * total, axis=1, keepdims=True)
            nall[q, 0, :, cols] = (total * gain[:, cols]).astype(BF16)
        squares[q] = square
        gathers[q] = [
            remote(nall.at[q, 0], nall.at[q, d], ag_s.at[q, d - 1], ag_r.at[q, d - 1], tp_peer(d))
            for d in (6, 4, 2, 5, 7, 1, 3)
        ]

    square_copies, factor_copies = {}, {}

    def share_squares(half):
        both = [jnp.broadcast_to(squares[2 * half + e], (16, 128)) for e in (0, 1)]
        sqall[half, 0] = jnp.concatenate(both * 4, axis=0).T[:8]
        square_copies[half] = [
            remote(sqall.at[half, 0], sqall.at[half, n + 1], sq_s.at[half, n], sq_r.at[half, n], peer(*other))
            for n, other in enumerate(others)
        ]

    def share_factor(half):
        for copy in square_copies[half]:
            copy.wait_recv()
        total = sqall[half, 0]
        for n in range(15):
            total = total + sqall[half, n + 1]
        fall[half, 0] = lax.rsqrt(total / D + 1e-05)
        factor_copies[half] = [
            remote(fall.at[half, 0], fall.at[half, d], fac_s.at[half, d - 1], fac_r.at[half, d - 1], tp_peer(d))
            for d in range(1, 8)
        ]

    rels = [(ic, i1, i3) for ic in (0, 1) for i1 in (0, 1) for i3 in (0, 1)]

    def owner(ic, i1, i3):
        return flip(c, ic) * 4 + xor_x(x, i1 ^ (3 * i3))

    def arrange(q):
        for copy in gathers[q]:
            copy.wait_recv()
        for n, rel in enumerate(rels):
            xp[q, n] = nall[q, owner(*rel)]

    core_out, red_out, gat_out, gco_out = {}, {}, {}, {}
    factors, final = {}, {}

    def multiply(u):
        q, first, count, _ = UNITS[u]
        if u == 0:
            for copy in got_gu:
                copy.wait()
        if u == FIRST[q]:
            arrange(q)
        rows = xp.at[q]
        for k in (0, 1):

            def tile(src, dst, width, k=k):
                prod = jnp.dot(rows[...].reshape(128, WIDE), gu[k, :, pl.ds(src, width)], preferred_element_type=F32)
                parts[u][:, :, :, :, pl.ds(dst, width)] = prod.astype(BF16).reshape(2, 2, 2, 16, width)

            def step(n, carry, k=k, tile=tile):
                src = pl.multiple_of(first * LANES + n * TILE, LANES)
                tile(src, pl.multiple_of(k * count * LANES + n * TILE, LANES), TILE)
                return carry

            lax.fori_loop(0, count // 2, step, 0, unroll=True)
            if count % 2:
                tile((first + count - 1) * LANES, (k * count + count - 1) * LANES, LANES)
        core_out[u] = remote(parts[u].at[1], crecs[u], core_s.at[u], core_r.at[u], peer(1, 0, 0))

    def summed(u, k, bits, cols):
        order = UNITS[u][3]
        total = parts[u][(0, *bits, slice(None), cols)].astype(F32)
        total = total + crecs[u][(*bits, slice(None), cols)].astype(F32)
        if k > 0:
            total = total + rec0[u][bits[order[1]], :, cols].astype(F32)
        if k > 1:
            total = total + rec1[u][:, cols].astype(F32)
        return total

    def reduce_step(u, k):
        _, _, count, order = UNITS[u]
        if k == 0:
            core_out[u].wait_recv()
        else:
            red_out[u, k - 1].wait_recv()
        index = pick(order, k) if k < 2 else (0, 0)
        for bits in blocks(index):
            for first, n in pieces(0, 2 * count):
                cols = lanes(first, n)
                total = summed(u, k, bits, cols)
                parts[u][(0, *bits, slice(None), cols)] = total.astype(BF16)
        device = step_peer[order[k]] if k < 2 else peer(0, 0, 1)
        red_out[u, k] = remote(
            parts[u].at[(0, *index)], (rec0, rec1, rec2)[k][u], red_s.at[u, k], red_r.at[u, k], device
        )

    def factor(q):
        half = q // 2
        if half not in factors:
            for copy in factor_copies[half]:
                copy.wait_recv()
            factors[half] = jnp.broadcast_to(fall[half, owner(0, 0, 0)][:1], (128, 128)).T
        return factors[half][q % 2 * 16 : q % 2 * 16 + 16]

    def activate(u):
        q, first, count, order = UNITS[u]
        red_out[u, 2].wait_recv()
        scales = factor(q)
        for n in range(count):
            gate, up = (
                (parts[u][0, 0, 0, :, lanes(n + k * count, 1)].astype(F32) + rec2[u][:, lanes(n + k * count, 1)].astype(F32))
                * scales
                for k in (0, 1)
            )
            act[q, 0, 0, 0, :, lanes(first + n, 1)] = (gate / (1.0 + jnp.exp(-gate)) * up).astype(BF16)
        gather_step(u, 1)

    def gather_step(u, k):
        q, first, count, order = UNITS[u]
        if k == 0:
            gat_out[u, 1].wait_recv()
        cols = pl.ds(first * LANES, count * LANES)
        gat_out[u, k] = remote(
            act.at[(q, 0, *pick(order, k, 0), slice(None), cols)],
            act.at[(q, 0, *pick(order, k, 1), slice(None), cols)],
            gat_s.at[u, k],
            gat_r.at[u, k],
            step_peer[order[k]],
        )

    def gather_core(u):
        q, first, count, _ = UNITS[u]
        gat_out[u, 0].wait_recv()
        index = (slice(None),) * 3 + (pl.ds(first * LANES, count * LANES),)
        gco_out[u] = remote(
            act.at[(q, 0, *index)], act.at[(q, 1, *index)], gco_s.at[u], gco_r.at[u], peer(1, 0, 0)
        )

    def down(q):
        for u in range(NU):
            if UNITS[u][0] == q:
                gco_out[u].wait_recv()
        if q == 0:
            for copy in got_dw:
                copy.wait()

        def tile(n, carry):
            cols = pl.ds(pl.multiple_of(n * TILE, TILE), TILE)
            prod = jnp.dot(act[q].reshape(128, FF), dw[:, cols], preferred_element_type=F32).astype(BF16)
            for i, rel in enumerate(rels):
                obuf[q, owner(*rel), :, cols] = prod[i * 16 : (i + 1) * 16]
            return carry

        lax.fori_loop(0, WIDE // TILE, tile, 0, unroll=True)
        final[q] = [
            remote(obuf.at[q, d], orec.at[q, d - 1], rs2_s.at[q, d - 1], rs2_r.at[q, d - 1], tp_peer(d))
            for d in (6, 4, 2, 5, 7, 1, 3)
        ]

    def finish(q):
        for copy in final[q]:
            copy.wait_recv()
        for n in range(WIDE // TILE):
            cols = slice(n * TILE, (n + 1) * TILE)
            total = hid[q, :, cols] + obuf[q, 0, :, cols].astype(F32)
            for d in range(7):
                total = total + orec[q, d, :, cols].astype(F32)
            result[rows_of(q), cols] = total.astype(BF16)

    attention(0)
    attention(1)
    pass_on(0)
    got_ow.wait()
    project(0)
    project(1)
    pass_on(1)
    project(2)
    project(3)
    actions = (
        multiply,
        lambda u: reduce_step(u, 0),
        lambda u: reduce_step(u, 1),
        lambda u: reduce_step(u, 2),
        activate,
        lambda u: gather_step(u, 0),
        gather_core,
    )
    steps = {'P': add_up, 'S': share_squares, 'T': share_factor, 'D': down, 'F': finish}
    for step, n in ORDER:
        (actions[step] if isinstance(step, int) else steps[step])(n)
    for copy in pending:
        copy.wait_send()


def on_device(query, new_kv, cache, lengths, out_weight, residual, norm_gain, gate_up, down_weight):
    vmem, smem, hbm = (pl.BlockSpec(memory_space=s) for s in (pltpu.VMEM, pltpu.SMEM, pl.ANY))
    dma = pltpu.SemaphoreType.DMA
    widths = [2 * LANES * count for _, _, count, _ in UNITS]
    scratch = [
        pltpu.VMEM((ROWS, HEADS, HD), F32),
        pltpu.VMEM((ROWS, HEADS, HD), F32),
        pltpu.VMEM((ROWS, HEADS, HD), F32),
        pltpu.VMEM((ROWS, HEADS, HD), F32),
        pltpu.VMEM((ROWS, SPAN, HD), BF16),
        pltpu.VMEM((ROWS, SPAN, HD), BF16),
        pltpu.VMEM((1024, WIDE), BF16),
        pltpu.VMEM((2, WIDE, FF), BF16),
        pltpu.VMEM((FF, WIDE), BF16),
        pltpu.VMEM((2, 2, 8, 16, 1024), BF16),
        pltpu.VMEM((QUARTERS, 8, 16, WIDE), BF16),
        pltpu.VMEM((QUARTERS, 7, 16, WIDE), BF16),
        pltpu.VMEM((QUARTERS, 16, WIDE), F32),
        pltpu.VMEM((2, 16, 8, 128), F32),
        pltpu.VMEM((2, 8, 8, 128), F32),
        pltpu.VMEM((QUARTERS, 8, 16, WIDE), BF16),
        pltpu.VMEM((QUARTERS, 8, 16, WIDE), BF16),
        pltpu.VMEM((QUARTERS, 2, 2, 2, 16, FF), BF16),
        pltpu.VMEM((QUARTERS, 8, 16, WIDE), BF16),
        pltpu.VMEM((QUARTERS, 7, 16, WIDE), BF16),
    ]
    scratch += [pltpu.VMEM((2, 2, 2, 16, w), BF16) for w in widths]
    scratch += [pltpu.VMEM((2, 2, 16, w), BF16) for w in widths]
    scratch += [pltpu.VMEM((2, 16, w), BF16) for w in widths]
    scratch += [pltpu.VMEM((16, w), BF16) for w in widths]
    scratch += [pltpu.VMEM((16, w), BF16) for w in widths]
    scratch += [dma((16,))]
    for shape in (
        (2, 7), (2, 8), (4, 7), (2, 15), (2, 7), (4, 7), (NU,), (NU, 3), (NU, 2), (NU,), (4, 7),
    ):
        scratch += [dma(shape), dma(shape)]
    return pl.pallas_call(
        body,
        out_shape=jax.ShapeDtypeStruct((64, WIDE), BF16),
        in_specs=[smem, vmem, vmem, vmem, vmem, hbm, hbm, hbm, hbm],
        out_specs=vmem,
        scratch_shapes=scratch,
        compiler_params=pltpu.CompilerParams(
            collective_id=0, has_side_effects=True, vmem_limit_bytes=63 * 2**20
        ),
        cost_estimate=pl.CostEstimate(flops=11_600_000_000, bytes_accessed=27_000_000, transcendentals=1_000_000),
    )(lengths, query, new_kv, residual, norm_gain.reshape(1, WIDE), cache, out_weight, gate_up, down_weight)


def solution(mesh):
    in_specs = (
        P(("pool", "grp"), "tp"),
        P(None, ("pool", "grp"), "tp"),
        P(None, ("pool", "grp"), "tp", None, None),
        P(("pool", "grp")),
        P("tp", ("pool", "grp")),
        P("tp", ("pool", "grp")),
        P(("pool", "grp")),
        P(None, ("pool", "grp"), "tp"),
        P("tp", ("pool", "grp")),
    )
    return jax.shard_map(
        on_device, mesh=mesh, in_specs=in_specs, out_specs=P("tp", ("pool", "grp")), check_vma=False
    )
```
